128 devices in a mesh: depth: 4 (over z_lo, core), row: 4 (over x), col: 8 (over z_hi, y).
Axes of the slice: x: 4, y: 4, z: 4 (z_hi: 2, z_lo: 2; z = z_hi * 2 + z_lo), core: 2. Of those that a mesh axis runs over, the one named last changes fastest.
Arguments:
- hidden: bfloat16 [2048, 26624], P(('depth', 'row'), 'col'), may hold values from -6 to 6
- grad_out: bfloat16 [2048, 8192], P(('depth', 'col'), 'row'), may hold values from -6 to 6
- weight: bfloat16 [26624, 8192], P('col', 'row'), may hold values from -0.0390625 to 0.0390625
Outputs:
- hidden_gradient: bfloat16 [2048, 26624], P(('depth', 'row'), 'col')
- down_matrix_derivative: bfloat16 [26624, 8192], P('col', ('depth', 'row'))
The draws below stay inside these ranges and needn't reach their ends.
All inputs are finite; a program needn't handle non-finite values.
Results may differ from the reference program's by a relative error of at most 0.005.
Values may be sent and summed in bfloat16 or wider, within the bound.
A program may use at most 128 MiB of HBM per device.

```python
import jax
import jax.numpy as jnp
from jax import lax

D = 8192
FF = 26624
SLAB = 512
TOKENS = 2048
N_DEPTH = 4


def block_levels(stream_key, shape, shards, least, top_value):
    gain, own = 1.0, jax.random.fold_in(stream_key, 6)
    for axis_at, parts in shards:
        draws = jnp.exp(jax.random.uniform(jax.random.fold_in(own, axis_at), (parts,), jnp.float32, least / len(shards), top_value / len(shards)))
        gain = gain * jnp.repeat(draws, shape[axis_at] // parts).reshape([-1 if axis == axis_at else 1 for axis in range(len(shape))])
    return gain


def gaussian(rng, extent, scale, reach, pieces=(), kind=jnp.bfloat16):
    array = jax.random.normal(rng, extent, jnp.float32) * scale
    if len(pieces) > 0:
        array = block_levels(rng, extent, pieces, -0.22, 0.18) * array
    return jnp.clip(array, min=-reach, max=reach).astype(kind)


def setup_inputs(seed: int = 0) -> dict:
    splits = jax.random.split(jax.random.key(seed), 4)
    hidden = gaussian(splits[0], (TOKENS, FF), 1.0, 6.0, ((0, 16), (1, 8)))
    grad_out = gaussian(splits[1], (TOKENS, D), 1.0, 6.0, ((0, 32), (1, 4)))
    weight = gaussian(splits[2], (FF, D), FF ** -0.5, 0.0390625, ((0, 8), (1, 4)))
    return {"hidden": hidden, "grad_out": grad_out, "weight": weight}


def reference(hidden, grad_out, weight):
    hidden_gradient = lax.dot_general(grad_out, weight, (((1,), (1,)), ((), ())), preferred_element_type=jnp.float32).astype(jnp.bfloat16)
    derivative_multiplier = TOKENS ** -0.5

    def add_slab(accumulator, token_slab_index):
        h_rows = lax.dynamic_slice_in_dim(hidden, token_slab_index * SLAB, SLAB, 0)
        g_rows = lax.dynamic_slice_in_dim(grad_out, token_slab_index * SLAB, SLAB, 0)
        partial_value = lax.dot_general(h_rows, g_rows, (((0,), (0,)), ((), ())), preferred_element_type=jnp.float32)
        partial_value = (partial_value * derivative_multiplier).astype(jnp.bfloat16)
        partial_value = lax.optimization_barrier(partial_value)
        return accumulator + partial_value.astype(jnp.float32), None

    accumulator, _ = lax.scan(add_slab, jnp.zeros((FF, D), jnp.float32), jnp.arange(N_DEPTH, dtype=jnp.int32))
    return hidden_gradient, accumulator.astype(jnp.bfloat16)
```

```python
import jax
import jax.numpy as jnp
from jax import lax
from jax.experimental import pallas as pl
from jax.experimental.pallas import tpu as pltpu
from jax.sharding import PartitionSpec as P

MESH = pl.DeviceIdType.MESH
BF16 = jnp.bfloat16
F32 = jnp.float32

T, F, U, M = 128, 3328, 64, 2048
SUB = M // 4
HALF = T // 2
TILE = 256
B_LO, B_HI = 16, 32
B0, B1 = HALF - B_LO, HALF + B_HI
LO, HI = (0, HALF), (HALF, T)
ALO, B, AHI = (0, B0), (B0, B1), (B1, T)
BLO, BHI = (B0, HALF), (HALF, B1)
SCALE = 2048.0 ** -0.5


def slot(dz, dk, dx):
    return dk * 4 + dx if dz == 0 else 8 + ((dx + 1) % 4) * 2 + dk


def kernel(
    h_ref, g_ref, w_ref, hg_ref, dw_ref,
    hb, wv, g1, st, g2, own, pb, r1, r2, acc, dwv, hgv,
    ssem, rsem, a2s, a2r, lsem, osem,
):
    d, r, c = lax.axis_index("depth"), lax.axis_index("row"), lax.axis_index("col")
    zl, k, zh, y = d // 2, d % 2, c // 4, c % 4
    xp, xm = (d, (r + 1) % 4, c), (d, (r + 3) % 4, c)
    zp, sib = ((1 - zl) * 2 + k, r, c), (zl * 2 + 1 - k, r, c)
    ys = [(d, r, zh * 4 + (y + i) % 4) for i in (1, 2, 3)]
    zhp = (d, r, (1 - zh) * 4 + y)

    def place(col, row):
        return ((col // 2 + 4 - row) % 4) * 2 + col % 2

    mine, other = place(c, r), place((1 - zh) * 4 + y, r)
    same = d == r

    local = [
        pltpu.make_async_copy(w_ref, wv, lsem.at[0]),
        pltpu.make_async_copy(h_ref, hb.at[slot(0, 0, 0)], lsem.at[1]),
        pltpu.make_async_copy(g_ref, g1.at[mine], lsem.at[2]),
    ]
    for cp in reversed(local):
        cp.start()

    barrier = pltpu.get_barrier_semaphore()
    for who in [xp, xm, zp, sib, zhp] + ys:
        pl.semaphore_signal(barrier, inc=1, device_id=who, device_id_type=MESH)
    for i in range(4):
        source = ((d + i) % 4, d, c)
        if i == 0:
            @pl.when(jnp.logical_not(same))
            def _():
                pl.semaphore_signal(barrier, inc=1, device_id=source, device_id_type=MESH)
        else:
            pl.semaphore_signal(barrier, inc=1, device_id=source, device_id_type=MESH)
    pl.semaphore_wait(barrier, 12 - same.astype(jnp.int32))

    copies = {}

    def send(key, src, dst, to):
        n = len(copies)
        cp = pltpu.make_async_remote_copy(
            src_ref=src, dst_ref=dst, send_sem=ssem.at[n], recv_sem=rsem.at[n],
            device_id=to, device_id_type=MESH,
        )
        cp.start()
        copies[key] = cp

    def got(*keys):
        for key in keys:
            copies[key].wait_recv()

    def rows(s, span):
        return hb.at[s, pl.ds(span[0], span[1] - span[0])]

    def pass_on(name, to, src, dst, span):
        send((name, dst, span), rows(src, span), rows(dst, span), to)

    rel = ((zl + r // 2) % 2) * 2 + (k + r % 2) % 2
    a2a = []
    for i in range(4):
        j = (r + i) % 4
        src = g_ref.at[:, pl.ds(pl.multiple_of(j * SUB, SUB), SUB)]
        dst = st.at[place(c, j), rel]
        cp = pltpu.make_async_remote_copy(
            src_ref=src, dst_ref=dst, send_sem=a2s.at[i], recv_sem=a2r.at[rel],
            device_id=(r, j, c), device_id_type=MESH,
        )
        a2a.append(cp)
        if i == 0:
            @pl.when(jnp.logical_not(same))
            def _():
                cp.start()

            @pl.when(same)
            def _():
                pltpu.make_async_copy(src, dst, a2r.at[0]).start()
        else:
            cp.start()

    send("g1z", g_ref, g1.at[mine], zhp)
    for i in range(3):
        send(("g1y", i), g_ref, g1.at[mine], ys[i])

    def h_own(name, to, dst, span):
        send((name, dst, span), h_ref.at[pl.ds(span[0], span[1] - span[0])], rows(dst, span), to)

    h_own("z", zp, slot(1, 0, 0), B)
    h_own("x", xp, slot(0, 0, 3), LO)
    h_own("x", xm, slot(0, 0, 1), HI)
    h_own("x", xp, slot(0, 0, 3), HI)
    h_own("x", xm, slot(0, 0, 1), LO)
    h_own("z", zp, slot(1, 0, 0), ALO)
    h_own("z", zp, slot(1, 0, 0), AHI)
    h_own("s", sib, slot(0, 1, 0), (0, T))

    got("g1z")
    for i in range(3):
        send(("g1zy", i), g1.at[other], g1.at[other], ys[i])

    for i in range(4):
        pltpu.make_async_copy(st.at[0, i], st.at[0, i], a2r.at[i]).wait()
    send("g2z", st.at[mine], st.at[mine], zhp)
    for i in range(3):
        send(("g2y", i), st.at[mine], st.at[mine], ys[i])

    def near(dx, half, part, to):
        s = slot(0, 0, dx)
        got(("x", s, half))
        if to is not None:
            pass_on("x", to, s, slot(0, 0, 2), half)
        pass_on("z", zp, s, slot(1, 0, dx), part)
        pass_on("s", sib, s, slot(0, 1, dx), half)

    near(3, LO, ALO, xp)
    near(1, HI, AHI, xm)

    got("g2z")
    for i in range(3):
        send(("g2zy", i), st.at[other], st.at[other], ys[i])

    got(("z", slot(1, 0, 0), B))
    pass_on("x", xp, slot(1, 0, 0), slot(1, 0, 3), B)
    pass_on("x", xm, slot(1, 0, 0), slot(1, 0, 1), B)

    near(3, HI, AHI, None)
    near(1, LO, ALO, None)

    local[0].wait()
    local[2].wait()
    got(*[("g1y", i) for i in range(3)], *[("g1zy", i) for i in range(3)])

    @pl.loop(0, F // TILE)
    def _(n):
        at = pl.ds(pl.multiple_of(n * TILE, TILE), TILE)
        p = lax.dot_general(
            g1[...].reshape(8 * U, M), wv[at, :], (((1,), (1,)), ((), ())),
            preferred_element_type=F32,
        )
        own[:, at] = p[:T]
        for j in range(3):
            pb[j, :, at] = p[T * (j + 1) : T * (j + 2)].astype(BF16)

    lo, hi = pl.ds(0, HALF), pl.ds(HALF, HALF)
    send("r1lo", pb.at[1, lo], r1.at[0], xm)
    send("r1hi", pb.at[1, hi], r1.at[1], xp)
    send("r2alo", pb.at[0, lo], r2.at[0, lo], xp)
    send("r2bhi", pb.at[2, hi], r2.at[1, hi], xm)

    s = slot(0, 0, 2)
    for half, part in ((LO, ALO), (HI, AHI)):
        got(("x", s, half))
        pass_on("z", zp, s, slot(1, 0, 2), part)
        pass_on("s", sib, s, slot(0, 1, 2), half)

    got(("z", slot(1, 0, 0), ALO), ("z", slot(1, 0, 0), AHI))
    pass_on("s", sib, slot(1, 0, 0), slot(1, 1, 0), (0, T))

    got(("x", slot(1, 0, 3), B))
    pass_on("x", xp, slot(1, 0, 3), slot(1, 0, 2), BLO)
    got(("x", slot(1, 0, 1), B))
    pass_on("x", xm, slot(1, 0, 1), slot(1, 0, 2), BHI)

    got("r1lo")
    pb[2, lo, :] = (pb[2, lo, :].astype(F32) + r1[0].astype(F32)).astype(BF16)
    send("r2blo", pb.at[2, lo], r2.at[1, lo], xm)
    got("r1hi")
    pb[0, hi, :] = (pb[0, hi, :].astype(F32) + r1[1].astype(F32)).astype(BF16)
    send("r2ahi", pb.at[0, hi], r2.at[0, hi], xp)

    got(*[("g2y", i) for i in range(3)], *[("g2zy", i) for i in range(3)])
    for dz in range(2):
        for dk in range(2):
            for dx in range(4):
                for half in range(2):
                    g2[slot(dz, dk, dx), half * U : (half + 1) * U, :] = st[dx * 2 + half, dz * 2 + dk]

    def product(first, last, at):
        depth = (last - first) * T
        return lax.dot_general(
            hb[first:last, :, at].reshape(depth, TILE), g2[first:last].reshape(depth, SUB),
            (((0,), (0,)), ((), ())), preferred_element_type=F32,
        )

    local[1].wait()
    got(("s", slot(0, 1, 0), (0, T)))
    for dx in (1, 2, 3):
        got(("s", slot(0, 1, dx), LO), ("s", slot(0, 1, dx), HI))

    @pl.loop(0, F // TILE)
    def _(n):
        at = pl.ds(pl.multiple_of(n * TILE, TILE), TILE)
        acc[at, :] = product(0, 8, at)

    for dx in (3, 1):
        got(("z", slot(1, 0, dx), ALO), ("z", slot(1, 0, dx), AHI))
        pass_on("s", sib, slot(1, 0, dx), slot(1, 1, dx), (0, T))

    got("r2alo", "r2bhi", "r2blo", "r2ahi")
    hgv[...] = (own[...] + r2[0].astype(F32) + r2[1].astype(F32)).astype(BF16)
    hg_copy = pltpu.make_async_copy(hgv, hg_ref, lsem.at[3])
    hg_copy.start()

    for dx in (0, 1, 3):
        got(("s", slot(1, 1, dx), (0, T)))

    @pl.loop(0, F // TILE)
    def _(n):
        at = pl.ds(pl.multiple_of(n * TILE, TILE), TILE)
        acc[at, :] += product(8, 14, at)

    s = slot(1, 0, 2)
    for name, part in (("x", BLO), ("x", BHI), ("z", ALO), ("z", AHI)):
        got((name, s, part))
        pass_on("s", sib, s, slot(1, 1, 2), part)
    for part in (BLO, BHI, ALO, AHI):
        got(("s", slot(1, 1, 2), part))

    @pl.loop(0, F // TILE)
    def _(n):
        at = pl.ds(pl.multiple_of(n * TILE, TILE), TILE)
        dwv[at, :] = ((acc[at, :] + product(14, 16, at)) * SCALE).astype(BF16)
        pltpu.make_async_copy(dwv.at[at], dw_ref.at[at], osem.at[n]).start()

    @pl.loop(0, F // TILE)
    def _(n):
        at = pl.ds(pl.multiple_of(n * TILE, TILE), TILE)
        pltpu.make_async_copy(dwv.at[at], dw_ref.at[at], osem.at[n]).wait()

    hg_copy.wait()
    for cp in copies.values():
        cp.wait_send()
    for i in range(1, 4):
        a2a[i].wait_send()

    @pl.when(jnp.logical_not(same))
    def _():
        a2a[0].wait_send()


def shards(hidden, grad_out, weight):
    return pl.pallas_call(
        kernel,
        out_shape=(jax.ShapeDtypeStruct((T, F), BF16), jax.ShapeDtypeStruct((F, SUB), BF16)),
        in_specs=[pl.BlockSpec(memory_space=pl.ANY)] * 3,
        out_specs=(pl.BlockSpec(memory_space=pl.ANY), pl.BlockSpec(memory_space=pl.ANY)),
        scratch_shapes=[
            pltpu.VMEM((16, T, F), BF16),
            pltpu.VMEM((F, M), BF16),
            pltpu.VMEM((8, U, M), BF16),
            pltpu.VMEM((8, 4, U, SUB), BF16),
            pltpu.VMEM((16, T, SUB), BF16),
            pltpu.VMEM((T, F), F32),
            pltpu.VMEM((3, T, F), BF16),
            pltpu.VMEM((2, HALF, F), BF16),
            pltpu.VMEM((2, T, F), BF16),
            pltpu.VMEM((F, SUB), F32),
            pltpu.VMEM((F, SUB), BF16),
            pltpu.VMEM((T, F), BF16),
            pltpu.SemaphoreType.DMA((64,)),
            pltpu.SemaphoreType.DMA((64,)),
            pltpu.SemaphoreType.DMA((4,)),
            pltpu.SemaphoreType.DMA((4,)),
            pltpu.SemaphoreType.DMA((4,)),
            pltpu.SemaphoreType.DMA((F // TILE,)),
        ],
        compiler_params=pltpu.CompilerParams(
            collective_id=0, has_side_effects=True, vmem_limit_bytes=60 * 2**20
        ),
        cost_estimate=pl.CostEstimate(
            flops=4 * 512 * M * F, bytes_accessed=2 * F * (M + SUB + 2 * T), transcendentals=0
        ),
    )(hidden, grad_out, weight)


def solution(mesh):
    return jax.shard_map(
        shards,
        mesh=mesh,
        in_specs=(P(("depth", "row"), "col"), P(("depth", "col"), "row"), P("col", "row")),
        out_specs=(P(("depth", "row"), "col"), P("col", ("depth", "row"))),
        check_vma=False,
    )
```

```python
import jax
import jax.numpy as jnp
from jax import lax
from jax.experimental import pallas as pl
from jax.experimental.pallas import tpu as pltpu
from jax.sharding import PartitionSpec as P

MESH = pl.DeviceIdType.MESH
BF16 = jnp.bfloat16
F32 = jnp.float32

T, F, U, M = 128, 3328, 64, 2048
SUB = M // 4
HALF = T // 2
TILE = 256
B_LO, B_HI = 16, 32
B0, B1 = HALF - B_LO, HALF + B_HI
LO, HI = (0, HALF), (HALF, T)
ALO, B, AHI = (0, B0), (B0, B1), (B1, T)
BLO, BHI = (B0, HALF), (HALF, B1)
SCALE = 2048.0 ** -0.5


def slot(dz, dk, dx):
    return dk * 4 + dx if dz == 0 else 8 + ((dx + 1) % 4) * 2 + dk


def kernel(
    h_ref, g_ref, w_ref, hg_ref, dw_ref,
    hb, wv, g1, st, g2, own, pb, r1, r2, acc, dwv, hgv,
    ssem, rsem, a2s, a2r, lsem, osem,
):
    d, r, c = lax.axis_index("depth"), lax.axis_index("row"), lax.axis_index("col")
    zl, k, zh, y = d // 2, d % 2, c // 4, c % 4
    xp, xm = (d, (r + 1) % 4, c), (d, (r + 3) % 4, c)
    zp, sib = ((1 - zl) * 2 + k, r, c), (zl * 2 + 1 - k, r, c)
    ys = [(d, r, zh * 4 + (y + i) % 4) for i in (1, 2, 3)]
    zhp = (d, r, (1 - zh) * 4 + y)

    def place(col, row):
        return ((col // 2 + 4 - row) % 4) * 2 + col % 2

    mine, other = place(c, r), place((1 - zh) * 4 + y, r)
    same = d == r

    local = [
        pltpu.make_async_copy(w_ref, wv, lsem.at[0]),
        pltpu.make_async_copy(h_ref, hb.at[slot(0, 0, 0)], lsem.at[1]),
        pltpu.make_async_copy(g_ref, g1.at[mine], lsem.at[2]),
    ]
    for cp in reversed(local):
        cp.start()

    barrier = pltpu.get_barrier_semaphore()
    for who in [xp, xm, zp, sib, zhp] + ys:
        pl.semaphore_signal(barrier, inc=1, device_id=who, device_id_type=MESH)
    for i in range(4):
        source = ((d + i) % 4, d, c)
        if i == 0:
            @pl.when(jnp.logical_not(same))
            def _():
                pl.semaphore_signal(barrier, inc=1, device_id=source, device_id_type=MESH)
        else:
            pl.semaphore_signal(barrier, inc=1, device_id=source, device_id_type=MESH)
    pl.semaphore_wait(barrier, 12 - same.astype(jnp.int32))

    copies = {}

    def send(key, src, dst, to):
        n = len(copies)
        cp = pltpu.make_async_remote_copy(
            src_ref=src, dst_ref=dst, send_sem=ssem.at[n], recv_sem=rsem.at[n],
            device_id=to, device_id_type=MESH,
        )
        cp.start()
        copies[key] = cp

    def got(*keys):
        for key in keys:
            copies[key].wait_recv()

    def rows(s, span):
        return hb.at[s, pl.ds(span[0], span[1] - span[0])]

    def pass_on(name, to, src, dst, span):
        send((name, dst, span), rows(src, span), rows(dst, span), to)

    rel = ((zl + r // 2) % 2) * 2 + (k + r % 2) % 2
    a2a = []
    for i in range(4):
        j = (r + i) % 4
        src = g_ref.at[:, pl.ds(pl.multiple_of(j * SUB, SUB), SUB)]
        dst = st.at[place(c, j), rel]
        cp = pltpu.make_async_remote_copy(
            src_ref=src, dst_ref=dst, send_sem=a2s.at[i], recv_sem=a2r.at[rel],
            device_id=(r, j, c), device_id_type=MESH,
        )
        a2a.append(cp)
        if i == 0:
            @pl.when(jnp.logical_not(same))
            def _():
                cp.start()

            @pl.when(same)
            def _():
                pltpu.make_async_copy(src, dst, a2r.at[0]).start()
        else:
            cp.start()

    send("g1z", g_ref, g1.at[mine], zhp)
    for i in range(3):
        send(("g1y", i), g_ref, g1.at[mine], ys[i])

    def h_own(name, to, dst, span):
        send((name, dst, span), h_ref.at[pl.ds(span[0], span[1] - span[0])], rows(dst, span), to)

    h_own("z", zp, slot(1, 0, 0), B)
    h_own("x", xp, slot(0, 0, 3), LO)
    h_own("x", xm, slot(0, 0, 1), HI)
    h_own("x", xp, slot(0, 0, 3), HI)
    h_own("x", xm, slot(0, 0, 1), LO)
    h_own("s", sib, slot(0, 1, 0), (0, T))

    got("g1z")
    for i in range(3):
        send(("g1zy", i), g1.at[other], g1.at[other], ys[i])

    for i in range(4):
        pltpu.make_async_copy(st.at[0, i], st.at[0, i], a2r.at[i]).wait()
    send("g2z", st.at[mine], st.at[mine], zhp)
    for i in range(3):
        send(("g2y", i), st.at[mine], st.at[mine], ys[i])
    h_own("z", zp, slot(1, 0, 0), ALO)
    h_own("z", zp, slot(1, 0, 0), AHI)

    def near(dx, half, part, to):
        s = slot(0, 0, dx)
        got(("x", s, half))
        if to is not None:
            pass_on("x", to, s, slot(0, 0, 2), half)
        pass_on("z", zp, s, slot(1, 0, dx), part)
        pass_on("s", sib, s, slot(0, 1, dx), half)

    near(3, LO, ALO, xp)
    near(1, HI, AHI, xm)

    got(("z", slot(1, 0, 0), B))
    pass_on("x", xp, slot(1, 0, 0), slot(1, 0, 3), B)
    pass_on("x", xm, slot(1, 0, 0), slot(1, 0, 1), B)

    near(3, HI, AHI, None)
    near(1, LO, ALO, None)

    local[0].wait()
    local[2].wait()
    got(*[("g1y", i) for i in range(3)], *[("g1zy", i) for i in range(3)])

    @pl.loop(0, F // TILE)
    def _(n):
        at = pl.ds(pl.multiple_of(n * TILE, TILE), TILE)
        p = lax.dot_general(
            g1[...].reshape(8 * U, M), wv[at, :], (((1,), (1,)), ((), ())),
            preferred_element_type=F32,
        )
        own[:, at] = p[:T]
        for j in range(3):
            pb[j, :, at] = p[T * (j + 1) : T * (j + 2)].astype(BF16)

    lo, hi = pl.ds(0, HALF), pl.ds(HALF, HALF)
    send("r1lo", pb.at[1, lo], r1.at[0], xm)
    send("r1hi", pb.at[1, hi], r1.at[1], xp)
    send("r2alo", pb.at[0, lo], r2.at[0, lo], xp)
    send("r2bhi", pb.at[2, hi], r2.at[1, hi], xm)

    got("g2z")
    for i in range(3):
        send(("g2zy", i), st.at[other], st.at[other], ys[i])

    s = slot(0, 0, 2)
    for half, part in ((LO, ALO), (HI, AHI)):
        got(("x", s, half))
        pass_on("z", zp, s, slot(1, 0, 2), part)
        pass_on("s", sib, s, slot(0, 1, 2), half)

    got(("z", slot(1, 0, 0), ALO), ("z", slot(1, 0, 0), AHI))
    pass_on("s", sib, slot(1, 0, 0), slot(1, 1, 0), (0, T))

    got(("x", slot(1, 0, 3), B))
    pass_on("x", xp, slot(1, 0, 3), slot(1, 0, 2), BLO)
    got(("x", slot(1, 0, 1), B))
    pass_on("x", xm, slot(1, 0, 1), slot(1, 0, 2), BHI)

    got(*[("g2y", i) for i in range(3)], *[("g2zy", i) for i in range(3)])
    for dz in range(2):
        for dk in range(2):
            for dx in range(4):
                for half in range(2):
                    g2[slot(dz, dk, dx), half * U : (half + 1) * U, :] = st[dx * 2 + half, dz * 2 + dk]

    def product(first, last, at):
        depth = (last - first) * T
        return lax.dot_general(
            hb[first:last, :, at].reshape(depth, TILE), g2[first:last].reshape(depth, SUB),
            (((0,), (0,)), ((), ())), preferred_element_type=F32,
        )

    local[1].wait()
    got(("s", slot(0, 1, 0), (0, T)))
    for dx in (1, 2, 3):
        got(("s", slot(0, 1, dx), LO), ("s", slot(0, 1, dx), HI))

    @pl.loop(0, F // TILE)
    def _(n):
        at = pl.ds(pl.multiple_of(n * TILE, TILE), TILE)
        acc[at, :] = product(0, 8, at)

    got("r1lo")
    pb[2, lo, :] = (pb[2, lo, :].astype(F32) + r1[0].astype(F32)).astype(BF16)
    send("r2blo", pb.at[2, lo], r2.at[1, lo], xm)
    got("r1hi")
    pb[0, hi, :] = (pb[0, hi, :].astype(F32) + r1[1].astype(F32)).astype(BF16)
    send("r2ahi", pb.at[0, hi], r2.at[0, hi], xp)

    for dx in (3, 1):
        got(("z", slot(1, 0, dx), ALO), ("z", slot(1, 0, dx), AHI))
        pass_on("s", sib, slot(1, 0, dx), slot(1, 1, dx), (0, T))

    for dx in (0, 1, 3):
        got(("s", slot(1, 1, dx), (0, T)))

    @pl.loop(0, F // TILE)
    def _(n):
        at = pl.ds(pl.multiple_of(n * TILE, TILE), TILE)
        acc[at, :] += product(8, 14, at)

    s = slot(1, 0, 2)
    for name, part in (("x", BLO), ("x", BHI), ("z", ALO), ("z", AHI)):
        got((name, s, part))
        pass_on("s", sib, s, slot(1, 1, 2), part)
    for part in (BLO, BHI, ALO, AHI):
        got(("s", slot(1, 1, 2), part))

    @pl.loop(0, F // TILE)
    def _(n):
        at = pl.ds(pl.multiple_of(n * TILE, TILE), TILE)
        dwv[at, :] = ((acc[at, :] + product(14, 16, at)) * SCALE).astype(BF16)
        pltpu.make_async_copy(dwv.at[at], dw_ref.at[at], osem.at[n]).start()

    got("r2alo", "r2bhi", "r2blo", "r2ahi")
    hgv[...] = (own[...] + r2[0].astype(F32) + r2[1].astype(F32)).astype(BF16)
    hg_copy = pltpu.make_async_copy(hgv, hg_ref, lsem.at[3])
    hg_copy.start()

    @pl.loop(0, F // TILE)
    def _(n):
        at = pl.ds(pl.multiple_of(n * TILE, TILE), TILE)
        pltpu.make_async_copy(dwv.at[at], dw_ref.at[at], osem.at[n]).wait()

    hg_copy.wait()
    for cp in copies.values():
        cp.wait_send()
    for i in range(1, 4):
        a2a[i].wait_send()

    @pl.when(jnp.logical_not(same))
    def _():
        a2a[0].wait_send()


def shards(hidden, grad_out, weight):
    return pl.pallas_call(
        kernel,
        out_shape=(jax.ShapeDtypeStruct((T, F), BF16), jax.ShapeDtypeStruct((F, SUB), BF16)),
        in_specs=[pl.BlockSpec(memory_space=pl.ANY)] * 3,
        out_specs=(pl.BlockSpec(memory_space=pl.ANY), pl.BlockSpec(memory_space=pl.ANY)),
        scratch_shapes=[
            pltpu.VMEM((16, T, F), BF16),
            pltpu.VMEM((F, M), BF16),
            pltpu.VMEM((8, U, M), BF16),
            pltpu.VMEM((8, 4, U, SUB), BF16),
            pltpu.VMEM((16, T, SUB), BF16),
            pltpu.VMEM((T, F), F32),
            pltpu.VMEM((3, T, F), BF16),
            pltpu.VMEM((2, HALF, F), BF16),
            pltpu.VMEM((2, T, F), BF16),
            pltpu.VMEM((F, SUB), F32),
            pltpu.VMEM((F, SUB), BF16),
            pltpu.VMEM((T, F), BF16),
            pltpu.SemaphoreType.DMA((64,)),
            pltpu.SemaphoreType.DMA((64,)),
            pltpu.SemaphoreType.DMA((4,)),
            pltpu.SemaphoreType.DMA((4,)),
            pltpu.SemaphoreType.DMA((4,)),
            pltpu.SemaphoreType.DMA((F // TILE,)),
        ],
        compiler_params=pltpu.CompilerParams(
            collective_id=0, has_side_effects=True, vmem_limit_bytes=60 * 2**20
        ),
        cost_estimate=pl.CostEstimate(
            flops=4 * 512 * M * F, bytes_accessed=2 * F * (M + SUB + 2 * T), transcendentals=0
        ),
    )(hidden, grad_out, weight)


def solution(mesh):
    return jax.shard_map(
        shards,
        mesh=mesh,
        in_specs=(P(("depth", "row"), "col"), P(("depth", "col"), "row"), P("col", "row")),
        out_specs=(P(("depth", "row"), "col"), P("col", ("depth", "row"))),
        check_vma=False,
    )
```

```python
import jax
import jax.numpy as jnp
from jax import lax
from jax.experimental import pallas as pl
from jax.experimental.pallas import tpu as pltpu
from jax.sharding import PartitionSpec as P

MESH = pl.DeviceIdType.MESH
BF16 = jnp.bfloat16
F32 = jnp.float32

T, F, U, M = 128, 3328, 64, 2048
SUB = M // 4
HALF = T // 2
TILE = 256
NW = 4
B_LO, B_HI = 16, 32
B0, B1 = HALF - B_LO, HALF + B_HI
LO, HI = (0, HALF), (HALF, T)
ALO, B, AHI = (0, B0), (B0, B1), (B1, T)
BLO, BHI = (B0, HALF), (HALF, B1)
COLS = ((0, 7 * TILE), (7 * TILE, F))
SCALE = 2048.0 ** -0.5


def slot(dz, dk, dx):
    return dk * 4 + dx if dz == 0 else 8 + (0, 1, 3, 2)[dx] * 2 + dk


def kernel(
    h_ref, g_ref, w_ref, hg_ref, dw_ref,
    hb, wv, g1, st, g2, own, pb, r1, r2, acc, dwv, hgv,
    ssem, rsem, a2s, a2r, lsem, osem, wsem,
):
    d, r, c = lax.axis_index("depth"), lax.axis_index("row"), lax.axis_index("col")
    zl, k, zh, y = d // 2, d % 2, c // 4, c % 4
    xp, xm = (d, (r + 1 + 2 * k) % 4, c), (d, (r + 3 - 2 * k) % 4, c)
    zp, sib = ((1 - zl) * 2 + k, r, c), (zl * 2 + 1 - k, r, c)
    yp, ym = (d, r, zh * 4 + (y + 1) % 4), (d, r, zh * 4 + (y + 3) % 4)
    zhp = (d, r, (1 - zh) * 4 + y)

    def place(col, row, core):
        return ((1 + 2 * core) * (col // 2 + 4 - row) % 4) * 2 + col % 2

    mine, other = place(c, r, k), place((1 - zh) * 4 + y, r, k)
    same = d == r

    local = [
        pltpu.make_async_copy(h_ref, hb.at[slot(0, 0, 0)], lsem.at[0]),
        pltpu.make_async_copy(g_ref, g1.at[mine], lsem.at[1]),
    ]
    for cp in reversed(local):
        cp.start()

    def weight_tile(n):
        at = pl.ds(pl.multiple_of(n * TILE, TILE), TILE)
        return pltpu.make_async_copy(w_ref.at[at], wv.at[n % NW], wsem.at[n % NW])

    for n in range(NW):
        weight_tile(n).start()

    barrier = pltpu.get_barrier_semaphore()
    for who in (xp, xm, zp, sib, zhp, yp, ym):
        pl.semaphore_signal(barrier, inc=1, device_id=who, device_id_type=MESH)
    for i in range(4):
        source = ((d + i) % 4, d, c)
        if i == 0:
            @pl.when(jnp.logical_not(same))
            def _():
                pl.semaphore_signal(barrier, inc=1, device_id=source, device_id_type=MESH)
        else:
            pl.semaphore_signal(barrier, inc=1, device_id=source, device_id_type=MESH)
    pl.semaphore_wait(barrier, 11 - same.astype(jnp.int32))

    copies = {}

    def send(key, src, dst, to):
        n = len(copies)
        cp = pltpu.make_async_remote_copy(
            src_ref=src, dst_ref=dst, send_sem=ssem.at[n], recv_sem=rsem.at[n],
            device_id=to, device_id_type=MESH,
        )
        cp.start()
        copies[key] = cp

    def got(*keys):
        for key in keys:
            if isinstance(key, tuple) and len(key) == 3:
                key = (*key, (0, F))
            copies[key].wait_recv()

    def rows(s, span, cols=(0, F)):
        return hb.at[s, pl.ds(span[0], span[1] - span[0]), pl.ds(cols[0], cols[1] - cols[0])]

    def pass_on(name, to, src, dst, span, cols=(0, F)):
        send((name, dst, span, cols), rows(src, span, cols), rows(dst, span, cols), to)

    rel = ((zl + r // 2) % 2) * 2 + (k + r % 2) % 2
    a2a = []
    for i in range(4):
        j = (r + i) % 4
        src = g_ref.at[:, pl.ds(pl.multiple_of(j * SUB, SUB), SUB)]
        dst = st.at[place(c, j, r % 2), rel]
        cp = pltpu.make_async_remote_copy(
            src_ref=src, dst_ref=dst, send_sem=a2s.at[i], recv_sem=a2r.at[rel],
            device_id=(r, j, c), device_id_type=MESH,
        )
        a2a.append(cp)
        if i == 0:
            @pl.when(jnp.logical_not(same))
            def _():
                cp.start()

            @pl.when(same)
            def _():
                pltpu.make_async_copy(src, dst, a2r.at[0]).start()
        else:
            cp.start()

    def ring(name, src, dst):
        send((name, "p"), src, dst, yp)
        send((name, "m"), src, dst, ym)

    def ring_on(name, buf, layer, n):
        for way, off, at, to in (("p", 3, 0, yp), ("m", 1, n, ym)):
            part = buf.at[place(layer * 4 + (y + off) % 4, r, k), pl.ds(at, n)]
            got((name, way))
            send((name, 2 * way), part, part, to)

    send("g1z", g_ref, g1.at[mine], zhp)
    ring("g1y", g_ref, g1.at[mine])

    def h_own(name, to, dst, span):
        send((name, dst, span, (0, F)), h_ref.at[pl.ds(span[0], span[1] - span[0])], rows(dst, span), to)

    h_own("z", zp, slot(1, 0, 0), B)
    h_own("x", xp, slot(0, 0, 3), LO)
    h_own("x", xm, slot(0, 0, 1), HI)
    h_own("x", xp, slot(0, 0, 3), HI)
    h_own("x", xm, slot(0, 0, 1), LO)
    h_own("s", sib, slot(0, 1, 0), (0, T))

    got("g1z")
    ring("g1zy", g1.at[other], g1.at[other])
    ring_on("g1y", g1, zh, U // 2)

    for i in range(4):
        pltpu.make_async_copy(st.at[0, i], st.at[0, i], a2r.at[i]).wait()
    send("g2z", st.at[mine], st.at[mine], zhp)
    h_own("z", zp, slot(1, 0, 0), ALO)
    h_own("z", zp, slot(1, 0, 0), AHI)

    def near(dx, half, part, to):
        s = slot(0, 0, dx)
        got(("x", s, half))
        if to is not None:
            pass_on("x", to, s, slot(0, 0, 2), half)
        pass_on("z", zp, s, slot(1, 0, dx), part)
        pass_on("s", sib, s, slot(0, 1, dx), half)

    near(3, LO, ALO, xp)
    near(1, HI, AHI, xm)

    ring_on("g1zy", g1, 1 - zh, U // 2)
    ring("g2y", st.at[mine], st.at[mine])

    got(("z", slot(1, 0, 0), B))
    pass_on("x", xp, slot(1, 0, 0), slot(1, 0, 3), B)
    pass_on("x", xm, slot(1, 0, 0), slot(1, 0, 1), B)

    near(3, HI, AHI, None)
    near(1, LO, ALO, None)

    local[1].wait()
    got(("g1y", "pp"), ("g1y", "mm"), ("g1zy", "pp"), ("g1zy", "mm"))

    def feature_sums(n):
        at = pl.ds(pl.multiple_of(n * TILE, TILE), TILE)
        weight_tile(n).wait()
        p = lax.dot_general(
            g1[...].reshape(8 * U, M), wv[n % NW], (((1,), (1,)), ((), ())),
            preferred_element_type=F32,
        )
        own[:, at] = p[:T]
        for j in range(3):
            pb[j, :, at] = p[T * (j + 1) : T * (j + 2)].astype(BF16)

        @pl.when(n + NW < F // TILE)
        def _():
            weight_tile(n + NW).start()

    pl.loop(0, 7)(feature_sums)
    got("g2z")
    ring("g2zy", st.at[other], st.at[other])

    pl.loop(7, F // TILE)(feature_sums)

    lo, hi = pl.ds(0, HALF), pl.ds(HALF, HALF)
    send("r1lo", pb.at[1, lo], r1.at[0], xm)
    send("r1hi", pb.at[1, hi], r1.at[1], xp)
    send("r2alo", pb.at[0, lo], r2.at[0, lo], xp)
    send("r2bhi", pb.at[2, hi], r2.at[1, hi], xm)

    ring_on("g2y", st, zh, 2)
    ring_on("g2zy", st, 1 - zh, 2)

    s = slot(0, 0, 2)
    for half in (LO, HI):
        got(("x", s, half))
        pass_on("s", sib, s, slot(0, 1, 2), half)
    for cols in COLS:
        for part in (ALO, AHI):
            pass_on("z", zp, s, slot(1, 0, 2), part, cols)

    got(("z", slot(1, 0, 0), ALO), ("z", slot(1, 0, 0), AHI))
    pass_on("s", sib, slot(1, 0, 0), slot(1, 1, 0), (0, T))

    got(("x", slot(1, 0, 3), B))
    pass_on("x", xp, slot(1, 0, 3), slot(1, 0, 2), BLO)
    got(("x", slot(1, 0, 1), B))
    pass_on("x", xm, slot(1, 0, 1), slot(1, 0, 2), BHI)

    got(("g2y", "pp"), ("g2y", "mm"), ("g2zy", "pp"), ("g2zy", "mm"))
    for dz in range(2):
        for dk in range(2):
            for dx in range(4):
                for half in range(2):
                    g2[slot(dz, dk, dx), half * U : (half + 1) * U, :] = st[(-dx if dk else dx) % 4 * 2 + half, dz * 2 + dk]

    def product(first, last, at):
        depth = (last - first) * T
        return lax.dot_general(
            hb[first:last, :, at].reshape(depth, TILE), g2[first:last].reshape(depth, SUB),
            (((0,), (0,)), ((), ())), preferred_element_type=F32,
        )

    local[0].wait()
    got(("s", slot(0, 1, 0), (0, T)))
    for dx in (1, 2, 3):
        got(("s", slot(0, 1, dx), LO), ("s", slot(0, 1, dx), HI))
    got(("s", slot(1, 1, 0), (0, T)))

    @pl.loop(0, F // TILE)
    def _(n):
        at = pl.ds(pl.multiple_of(n * TILE, TILE), TILE)
        acc[at, :] = product(0, 10, at)

    got("r1lo")
    pb[2, lo, :] = (pb[2, lo, :].astype(F32) + r1[0].astype(F32)).astype(BF16)
    send("r2blo", pb.at[2, lo], r2.at[1, lo], xm)
    got("r1hi")
    pb[0, hi, :] = (pb[0, hi, :].astype(F32) + r1[1].astype(F32)).astype(BF16)
    send("r2ahi", pb.at[0, hi], r2.at[0, hi], xp)

    for dx in (3, 1):
        got(("z", slot(1, 0, dx), ALO), ("z", slot(1, 0, dx), AHI))
        pass_on("s", sib, slot(1, 0, dx), slot(1, 1, dx), (0, T))

    for dx in (1, 3):
        got(("s", slot(1, 1, dx), (0, T)))

    @pl.loop(0, F // TILE)
    def _(n):
        at = pl.ds(pl.multiple_of(n * TILE, TILE), TILE)
        acc[at, :] += product(10, 14, at)

    s = slot(1, 0, 2)
    for part in (BLO, BHI):
        got(("x", s, part))
        pass_on("s", sib, s, slot(1, 1, 2), part)
    for cols in COLS:
        for part in (ALO, AHI):
            got(("z", s, part, cols))
            pass_on("s", sib, s, slot(1, 1, 2), part, cols)
        if cols == COLS[0]:
            got(("s", slot(1, 1, 2), BLO), ("s", slot(1, 1, 2), BHI))
        for part in (ALO, AHI):
            got(("s", slot(1, 1, 2), part, cols))

        @pl.loop(cols[0] // TILE, cols[1] // TILE)
        def _(n):
            at = pl.ds(pl.multiple_of(n * TILE, TILE), TILE)
            dwv[at, :] = ((acc[at, :] + product(14, 16, at)) * SCALE).astype(BF16)
            pltpu.make_async_copy(dwv.at[at], dw_ref.at[at], osem.at[n]).start()

    got("r2alo", "r2bhi")
    own[lo, :] += r2[0, lo, :].astype(F32)
    own[hi, :] += r2[1, hi, :].astype(F32)
    hg_copies = []
    for i, (name, half) in enumerate((("r2blo", lo), ("r2ahi", hi))):
        got(name)
        hgv[half, :] = (own[half, :] + r2[1 - i, half, :].astype(F32)).astype(BF16)
        hg_copies.append(pltpu.make_async_copy(hgv.at[half], hg_ref.at[half], lsem.at[2 + i]))
        hg_copies[i].start()

    @pl.loop(0, F // TILE)
    def _(n):
        at = pl.ds(pl.multiple_of(n * TILE, TILE), TILE)
        pltpu.make_async_copy(dwv.at[at], dw_ref.at[at], osem.at[n]).wait()

    for cp in hg_copies:
        cp.wait()
    for cp in copies.values():
        cp.wait_send()
    for i in range(1, 4):
        a2a[i].wait_send()

    @pl.when(jnp.logical_not(same))
    def _():
        a2a[0].wait_send()


def shards(hidden, grad_out, weight):
    hidden, grad_out, weight = (pltpu.with_memory_space_constraint(a, pltpu.HBM) for a in (hidden, grad_out, weight))
    return pl.pallas_call(
        kernel,
        out_shape=(jax.ShapeDtypeStruct((T, F), BF16), jax.ShapeDtypeStruct((F, SUB), BF16)),
        in_specs=[pl.BlockSpec(memory_space=pltpu.HBM)] * 3,
        out_specs=(pl.BlockSpec(memory_space=pl.ANY), pl.BlockSpec(memory_space=pl.ANY)),
        scratch_shapes=[
            pltpu.VMEM((16, T, F), BF16),
            pltpu.VMEM((NW, TILE, M), BF16),
            pltpu.VMEM((8, U, M), BF16),
            pltpu.VMEM((8, 4, U, SUB), BF16),
            pltpu.VMEM((16, T, SUB), BF16),
            pltpu.VMEM((T, F), F32),
            pltpu.VMEM((3, T, F), BF16),
            pltpu.VMEM((2, HALF, F), BF16),
            pltpu.VMEM((2, T, F), BF16),
            pltpu.VMEM((F, SUB), F32),
            pltpu.VMEM((F, SUB), BF16),
            pltpu.VMEM((T, F), BF16),
            pltpu.SemaphoreType.DMA((64,)),
            pltpu.SemaphoreType.DMA((64,)),
            pltpu.SemaphoreType.DMA((4,)),
            pltpu.SemaphoreType.DMA((4,)),
            pltpu.SemaphoreType.DMA((4,)),
            pltpu.SemaphoreType.DMA((F // TILE,)),
            pltpu.SemaphoreType.DMA((NW,)),
        ],
        compiler_params=pltpu.CompilerParams(
            collective_id=0, has_side_effects=True, vmem_limit_bytes=42 * 2**20
        ),
        cost_estimate=pl.CostEstimate(
            flops=4 * 512 * M * F, bytes_accessed=2 * F * (M + SUB + 2 * T), transcendentals=0
        ),
    )(hidden, grad_out, weight)


def solution(mesh):
    return jax.shard_map(
        shards,
        mesh=mesh,
        in_specs=(P(("depth", "row"), "col"), P(("depth", "col"), "row"), P("col", "row")),
        out_specs=(P(("depth", "row"), "col"), P("col", ("depth", "row"))),
        check_vma=False,
    )
```

```python
import jax
import jax.numpy as jnp
from jax import lax
from jax.experimental import pallas as pl
from jax.experimental.pallas import tpu as pltpu
from jax.sharding import PartitionSpec as P

MESH = pl.DeviceIdType.MESH
BF16 = jnp.bfloat16
F32 = jnp.float32

T, F, U, M = 128, 3328, 64, 2048
SUB = M // 4
HALF = T // 2
TILE = 256
NW = 4
B_LO, B_HI = 16, 32
B0, B1 = HALF - B_LO, HALF + B_HI
LO, HI = (0, HALF), (HALF, T)
ALO, B, AHI = (0, B0), (B0, B1), (B1, T)
BLO, BHI = (B0, HALF), (HALF, B1)
COLS = ((0, 7 * TILE), (7 * TILE, F))
SCALE = 2048.0 ** -0.5


def slot(dz, dk, dx):
    return dk * 4 + dx if dz == 0 else 8 + (0, 1, 3, 2)[dx] * 2 + dk


def kernel(
    h_ref, g_ref, w_ref, hg_ref, dw_ref,
    hb, wv, g1, st, g2, own, pb, r1, r2, acc,
    ssem, rsem, a2s, a2r, lsem, wsem,
):
    d, r, c = lax.axis_index("depth"), lax.axis_index("row"), lax.axis_index("col")
    zl, k, zh, y = d // 2, d % 2, c // 4, c % 4
    xp, xm = (d, (r + 1 + 2 * k) % 4, c), (d, (r + 3 - 2 * k) % 4, c)
    zp, sib = ((1 - zl) * 2 + k, r, c), (zl * 2 + 1 - k, r, c)
    yp, ym = (d, r, zh * 4 + (y + 1) % 4), (d, r, zh * 4 + (y + 3) % 4)
    zhp = (d, r, (1 - zh) * 4 + y)

    def place(col, row, core):
        return ((1 + 2 * core) * (col // 2 + 4 - row) % 4) * 2 + col % 2

    mine, other = place(c, r, k), place((1 - zh) * 4 + y, r, k)
    same = d == r

    local = [
        pltpu.make_async_copy(h_ref, hb.at[slot(0, 0, 0)], lsem.at[0]),
        pltpu.make_async_copy(g_ref, g1.at[mine], lsem.at[1]),
    ]
    for cp in reversed(local):
        cp.start()

    def weight_tile(n):
        at = pl.ds(pl.multiple_of(n * TILE, TILE), TILE)
        return pltpu.make_async_copy(w_ref.at[at], wv.at[n % NW], wsem.at[n % NW])

    for n in range(NW):
        weight_tile(n).start()

    barrier = pltpu.get_barrier_semaphore()
    for who in (xp, xm, zp, sib, zhp, yp, ym):
        pl.semaphore_signal(barrier, inc=1, device_id=who, device_id_type=MESH)
    for i in range(4):
        source = ((d + i) % 4, d, c)
        if i == 0:
            @pl.when(jnp.logical_not(same))
            def _():
                pl.semaphore_signal(barrier, inc=1, device_id=source, device_id_type=MESH)
        else:
            pl.semaphore_signal(barrier, inc=1, device_id=source, device_id_type=MESH)
    pl.semaphore_wait(barrier, 11 - same.astype(jnp.int32))

    copies = {}

    def send(key, src, dst, to):
        n = len(copies)
        cp = pltpu.make_async_remote_copy(
            src_ref=src, dst_ref=dst, send_sem=ssem.at[n], recv_sem=rsem.at[n],
            device_id=to, device_id_type=MESH,
        )
        cp.start()
        copies[key] = cp

    done = []

    def sent(n):
        for cp in list(copies.values())[len(done) : n]:
            cp.wait_send()
            done.append(cp)

    def got(*keys):
        for key in keys:
            if isinstance(key, tuple) and len(key) == 3:
                key = (*key, (0, F))
            copies[key].wait_recv()

    def rows(s, span, cols=(0, F)):
        return hb.at[s, pl.ds(span[0], span[1] - span[0]), pl.ds(cols[0], cols[1] - cols[0])]

    def pass_on(name, to, src, dst, span, cols=(0, F)):
        send((name, dst, span, cols), rows(src, span, cols), rows(dst, span, cols), to)

    rel = ((zl + r // 2) % 2) * 2 + (k + r % 2) % 2
    a2a = []
    for i in range(4):
        j = (r + i) % 4
        src = g_ref.at[:, pl.ds(pl.multiple_of(j * SUB, SUB), SUB)]
        dst = st.at[place(c, j, r % 2), rel]
        cp = pltpu.make_async_remote_copy(
            src_ref=src, dst_ref=dst, send_sem=a2s.at[i], recv_sem=a2r.at[rel],
            device_id=(r, j, c), device_id_type=MESH,
        )
        a2a.append(cp)
        if i == 0:
            @pl.when(jnp.logical_not(same))
            def _():
                cp.start()

            @pl.when(same)
            def _():
                pltpu.make_async_copy(src, dst, a2r.at[0]).start()
        else:
            cp.start()

    def ring(name, src, dst):
        send((name, "p"), src, dst, yp)
        send((name, "m"), src, dst, ym)

    def ring_on(name, buf, layer, n):
        for way, off, at, to in (("p", 3, 0, yp), ("m", 1, n, ym)):
            part = buf.at[place(layer * 4 + (y + off) % 4, r, k), pl.ds(at, n)]
            got((name, way))
            send((name, 2 * way), part, part, to)

    send("g1z", g_ref, g1.at[mine], zhp)
    ring("g1y", g_ref, g1.at[mine])

    def h_own(name, to, dst, span):
        send((name, dst, span, (0, F)), h_ref.at[pl.ds(span[0], span[1] - span[0])], rows(dst, span), to)

    h_own("z", zp, slot(1, 0, 0), B)
    h_own("x", xp, slot(0, 0, 3), LO)
    h_own("x", xm, slot(0, 0, 1), HI)
    h_own("x", xp, slot(0, 0, 3), HI)
    h_own("x", xm, slot(0, 0, 1), LO)
    h_own("s", sib, slot(0, 1, 0), (0, T))

    got("g1z")
    ring("g1zy", g1.at[other], g1.at[other])
    ring_on("g1y", g1, zh, U // 2)

    for i in range(4):
        pltpu.make_async_copy(st.at[0, i], st.at[0, i], a2r.at[i]).wait()
    send("g2z", st.at[mine], st.at[mine], zhp)
    h_own("z", zp, slot(1, 0, 0), ALO)
    h_own("z", zp, slot(1, 0, 0), AHI)

    def near(dx, half, part, to):
        s = slot(0, 0, dx)
        got(("x", s, half))
        if to is not None:
            pass_on("x", to, s, slot(0, 0, 2), half)
        pass_on("z", zp, s, slot(1, 0, dx), part)
        pass_on("s", sib, s, slot(0, 1, dx), half)

    near(3, LO, ALO, xp)
    near(1, HI, AHI, xm)

    ring_on("g1zy", g1, 1 - zh, U // 2)
    ring("g2y", st.at[mine], st.at[mine])

    got(("z", slot(1, 0, 0), B))
    pass_on("x", xp, slot(1, 0, 0), slot(1, 0, 3), B)
    pass_on("x", xm, slot(1, 0, 0), slot(1, 0, 1), B)

    near(3, HI, AHI, None)
    near(1, LO, ALO, None)

    local[1].wait()
    got(("g1y", "pp"), ("g1y", "mm"), ("g1zy", "pp"), ("g1zy", "mm"))

    def feature_sums(n):
        at = pl.ds(pl.multiple_of(n * TILE, TILE), TILE)
        weight_tile(n).wait()
        p = lax.dot_general(
            g1[...].reshape(8 * U, M), wv[n % NW], (((1,), (1,)), ((), ())),
            preferred_element_type=F32,
        )
        own[:, at] = p[:T]
        for j in range(3):
            pb[j, :, at] = p[T * (j + 1) : T * (j + 2)].astype(BF16)

        @pl.when(n + NW < F // TILE)
        def _():
            weight_tile(n + NW).start()

    pl.loop(0, 7)(feature_sums)
    got("g2z")
    ring("g2zy", st.at[other], st.at[other])

    pl.loop(7, F // TILE)(feature_sums)

    lo, hi = pl.ds(0, HALF), pl.ds(HALF, HALF)
    early = len(copies)
    send("r1lo", pb.at[1, lo], r1.at[0], xm)
    send("r1hi", pb.at[1, hi], r1.at[1], xp)
    send("r2alo", pb.at[0, lo], r2.at[0, lo], xp)
    send("r2bhi", pb.at[2, hi], r2.at[1, hi], xm)

    ring_on("g2y", st, zh, 2)
    ring_on("g2zy", st, 1 - zh, 2)

    s = slot(0, 0, 2)
    for half in (LO, HI):
        got(("x", s, half))
        pass_on("s", sib, s, slot(0, 1, 2), half)
    for cols in COLS:
        for part in (ALO, AHI):
            pass_on("z", zp, s, slot(1, 0, 2), part, cols)

    got(("z", slot(1, 0, 0), ALO), ("z", slot(1, 0, 0), AHI))
    pass_on("s", sib, slot(1, 0, 0), slot(1, 1, 0), (0, T))

    got(("x", slot(1, 0, 3), B))
    pass_on("x", xp, slot(1, 0, 3), slot(1, 0, 2), BLO)
    got(("x", slot(1, 0, 1), B))
    pass_on("x", xm, slot(1, 0, 1), slot(1, 0, 2), BHI)

    got(("g2y", "pp"), ("g2y", "mm"), ("g2zy", "pp"), ("g2zy", "mm"))
    for dz in range(2):
        for dk in range(2):
            for dx in range(4):
                for half in range(2):
                    g2[slot(dz, dk, dx), half * U : (half + 1) * U, :] = st[(-dx if dk else dx) % 4 * 2 + half, dz * 2 + dk]

    def product(first, last, at):
        depth = (last - first) * T
        return lax.dot_general(
            hb[first:last, :, at].reshape(depth, TILE), g2[first:last].reshape(depth, SUB),
            (((0,), (0,)), ((), ())), preferred_element_type=F32,
        )

    local[0].wait()
    got(("s", slot(0, 1, 0), (0, T)))
    for dx in (1, 2, 3):
        got(("s", slot(0, 1, dx), LO), ("s", slot(0, 1, dx), HI))
    got(("s", slot(1, 1, 0), (0, T)))

    @pl.loop(0, F // TILE)
    def _(n):
        at = pl.ds(pl.multiple_of(n * TILE, TILE), TILE)
        acc[at, :] = product(0, 10, at)

    got("r1lo")
    pb[2, lo, :] = (pb[2, lo, :].astype(F32) + r1[0].astype(F32)).astype(BF16)
    send("r2blo", pb.at[2, lo], r2.at[1, lo], xm)
    got("r1hi")
    pb[0, hi, :] = (pb[0, hi, :].astype(F32) + r1[1].astype(F32)).astype(BF16)
    send("r2ahi", pb.at[0, hi], r2.at[0, hi], xp)

    for dx in (3, 1):
        got(("z", slot(1, 0, dx), ALO), ("z", slot(1, 0, dx), AHI))
        pass_on("s", sib, slot(1, 0, dx), slot(1, 1, dx), (0, T))

    sent(early)
    for i in range(1, 4):
        a2a[i].wait_send()

    @pl.when(jnp.logical_not(same))
    def _():
        a2a[0].wait_send()

    for dx in (1, 3):
        got(("s", slot(1, 1, dx), (0, T)))

    @pl.loop(0, F // TILE)
    def _(n):
        at = pl.ds(pl.multiple_of(n * TILE, TILE), TILE)
        acc[at, :] += product(10, 14, at)

    s = slot(1, 0, 2)
    for part in (BLO, BHI):
        got(("x", s, part))
        pass_on("s", sib, s, slot(1, 1, 2), part)
    for cols in COLS:
        for part in (ALO, AHI):
            got(("z", s, part, cols))
            pass_on("s", sib, s, slot(1, 1, 2), part, cols)
        if cols == COLS[0]:
            got(("s", slot(1, 1, 2), BLO), ("s", slot(1, 1, 2), BHI))
        for part in (ALO, AHI):
            got(("s", slot(1, 1, 2), part, cols))

        @pl.loop(cols[0] // TILE, cols[1] // TILE)
        def _(n):
            at = pl.ds(pl.multiple_of(n * TILE, TILE), TILE)
            dw_ref[at, :] = ((acc[at, :] + product(14, 16, at)) * SCALE).astype(BF16)

    got("r2alo", "r2bhi")
    own[lo, :] += r2[0, lo, :].astype(F32)
    own[hi, :] += r2[1, hi, :].astype(F32)
    for i, (name, half) in enumerate((("r2blo", lo), ("r2ahi", hi))):
        got(name)
        hg_ref[half, :] = (own[half, :] + r2[1 - i, half, :].astype(F32)).astype(BF16)

    sent(len(copies))


def shards(hidden, grad_out, weight):
    hidden, grad_out, weight = (pltpu.with_memory_space_constraint(a, pltpu.HBM) for a in (hidden, grad_out, weight))
    return pl.pallas_call(
        kernel,
        out_shape=(jax.ShapeDtypeStruct((T, F), BF16), jax.ShapeDtypeStruct((F, SUB), BF16)),
        in_specs=[pl.BlockSpec(memory_space=pltpu.HBM)] * 3,
        out_specs=(pl.BlockSpec(memory_space=pltpu.VMEM), pl.BlockSpec(memory_space=pltpu.VMEM)),
        scratch_shapes=[
            pltpu.VMEM((16, T, F), BF16),
            pltpu.VMEM((NW, TILE, M), BF16),
            pltpu.VMEM((8, U, M), BF16),
            pltpu.VMEM((8, 4, U, SUB), BF16),
            pltpu.VMEM((16, T, SUB), BF16),
            pltpu.VMEM((T, F), F32),
            pltpu.VMEM((3, T, F), BF16),
            pltpu.VMEM((2, HALF, F), BF16),
            pltpu.VMEM((2, T, F), BF16),
            pltpu.VMEM((F, SUB), F32),
            pltpu.SemaphoreType.DMA((64,)),
            pltpu.SemaphoreType.DMA((64,)),
            pltpu.SemaphoreType.DMA((4,)),
            pltpu.SemaphoreType.DMA((4,)),
            pltpu.SemaphoreType.DMA((2,)),
            pltpu.SemaphoreType.DMA((NW,)),
        ],
        compiler_params=pltpu.CompilerParams(
            collective_id=0, has_side_effects=True, vmem_limit_bytes=44 * 2**20
        ),
        cost_estimate=pl.CostEstimate(
            flops=4 * 512 * M * F, bytes_accessed=2 * F * (M + SUB + 2 * T), transcendentals=0
        ),
    )(hidden, grad_out, weight)


def solution(mesh):
    return jax.shard_map(
        shards,
        mesh=mesh,
        in_specs=(P(("depth", "row"), "col"), P(("depth", "col"), "row"), P("col", "row")),
        out_specs=(P(("depth", "row"), "col"), P("col", ("depth", "row"))),
        check_vma=False,
    )
```

```python
import jax
import jax.numpy as jnp
from jax import lax
from jax.experimental import pallas as pl
from jax.experimental.pallas import tpu as pltpu
from jax.sharding import PartitionSpec as P

MESH = pl.DeviceIdType.MESH
BF16 = jnp.bfloat16
F32 = jnp.float32

T, F, U, M = 128, 3328, 64, 2048
SUB = M // 4
HALF = T // 2
TILE = 256
NW = 4
B_LO, B_HI = 16, 32
B0, B1 = HALF - B_LO, HALF + B_HI
LO, HI = (0, HALF), (HALF, T)
ALO, B, AHI = (0, B0), (B0, B1), (B1, T)
BLO, BHI = (B0, HALF), (HALF, B1)
COLS = ((0, 7 * TILE), (7 * TILE, F))
SCALE = 2048.0 ** -0.5


def slot(dz, dk, dx):
    return dk * 4 + dx if dz == 0 else 8 + (0, 1, 3, 2)[dx] * 2 + dk


def kernel(
    h_ref, g_ref, w_ref, hg_ref, dw_ref,
    hb, wv, g1, st, g2, own, pb, r1, r2, acc,
    ssem, rsem, a2s, a2r, lsem, wsem,
):
    d, r, c = lax.axis_index("depth"), lax.axis_index("row"), lax.axis_index("col")
    zl, k, zh, y = d // 2, d % 2, c // 4, c % 4
    xp, xm = (d, (r + 1 + 2 * k) % 4, c), (d, (r + 3 - 2 * k) % 4, c)
    zp, sib = ((1 - zl) * 2 + k, r, c), (zl * 2 + 1 - k, r, c)
    yp, ym = (d, r, zh * 4 + (y + 1) % 4), (d, r, zh * 4 + (y + 3) % 4)
    zhp = (d, r, (1 - zh) * 4 + y)

    def place(col, row, core):
        return ((1 + 2 * core) * (col // 2 + 4 - row) % 4) * 2 + col % 2

    mine, other = place(c, r, k), place((1 - zh) * 4 + y, r, k)
    same = d == r

    local = [
        pltpu.make_async_copy(h_ref, hb.at[slot(0, 0, 0)], lsem.at[0]),
        pltpu.make_async_copy(g_ref, g1.at[mine], lsem.at[1]),
    ]
    for cp in reversed(local):
        cp.start()

    def weight_tile(n):
        at = pl.ds(pl.multiple_of(n * TILE, TILE), TILE)
        return pltpu.make_async_copy(w_ref.at[at], wv.at[n % NW], wsem.at[n % NW])

    for n in range(NW):
        weight_tile(n).start()

    barrier = pltpu.get_barrier_semaphore()
    for who in (xp, xm, zp, sib, zhp, yp, ym):
        pl.semaphore_signal(barrier, inc=1, device_id=who, device_id_type=MESH)
    for i in range(4):
        source = ((d + i) % 4, d, c)
        if i == 0:
            @pl.when(jnp.logical_not(same))
            def _():
                pl.semaphore_signal(barrier, inc=1, device_id=source, device_id_type=MESH)
        else:
            pl.semaphore_signal(barrier, inc=1, device_id=source, device_id_type=MESH)
    pl.semaphore_wait(barrier, 11 - same.astype(jnp.int32))

    copies = {}

    def send(key, src, dst, to):
        n = len(copies)
        cp = pltpu.make_async_remote_copy(
            src_ref=src, dst_ref=dst, send_sem=ssem.at[n], recv_sem=rsem.at[n],
            device_id=to, device_id_type=MESH,
        )
        cp.start()
        copies[key] = cp

    done = []

    def sent(n):
        for cp in list(copies.values())[len(done) : n]:
            cp.wait_send()
            done.append(cp)

    def got(*keys):
        for key in keys:
            if isinstance(key, tuple) and len(key) == 3:
                key = (*key, (0, F))
            copies[key].wait_recv()

    def rows(s, span, cols=(0, F)):
        return hb.at[s, pl.ds(span[0], span[1] - span[0]), pl.ds(cols[0], cols[1] - cols[0])]

    def pass_on(name, to, src, dst, span, cols=(0, F)):
        send((name, dst, span, cols), rows(src, span, cols), rows(dst, span, cols), to)

    rel = ((zl + r // 2) % 2) * 2 + (k + r % 2) % 2
    a2a = []
    for i in range(4):
        j = (r + i) % 4
        src = g_ref.at[:, pl.ds(pl.multiple_of(j * SUB, SUB), SUB)]
        dst = st.at[place(c, j, r % 2), rel]
        cp = pltpu.make_async_remote_copy(
            src_ref=src, dst_ref=dst, send_sem=a2s.at[i], recv_sem=a2r.at[rel],
            device_id=(r, j, c), device_id_type=MESH,
        )
        a2a.append(cp)
        if i == 0:
            @pl.when(jnp.logical_not(same))
            def _():
                cp.start()

            @pl.when(same)
            def _():
                pltpu.make_async_copy(src, dst, a2r.at[0]).start()
        else:
            cp.start()

    def ring(name, src, dst):
        send((name, "p"), src, dst, yp)
        send((name, "m"), src, dst, ym)

    def ring_on(name, buf, layer, n):
        for way, off, at, to in (("p", 3, 0, yp), ("m", 1, n, ym)):
            part = buf.at[place(layer * 4 + (y + off) % 4, r, k), pl.ds(at, n)]
            got((name, way))
            send((name, 2 * way), part, part, to)

    send("g1z", g_ref, g1.at[mine], zhp)
    ring("g1y", g_ref, g1.at[mine])

    def h_own(name, to, dst, span):
        send((name, dst, span, (0, F)), h_ref.at[pl.ds(span[0], span[1] - span[0])], rows(dst, span), to)

    h_own("z", zp, slot(1, 0, 0), B)
    h_own("x", xp, slot(0, 0, 3), LO)
    h_own("x", xm, slot(0, 0, 1), HI)
    h_own("x", xp, slot(0, 0, 3), HI)
    h_own("x", xm, slot(0, 0, 1), LO)
    h_own("s", sib, slot(0, 1, 0), (0, T))

    got("g1z")
    ring("g1zy", g1.at[other], g1.at[other])
    ring_on("g1y", g1, zh, U // 2)

    for i in range(4):
        pltpu.make_async_copy(st.at[0, i], st.at[0, i], a2r.at[i]).wait()
    send("g2z", st.at[mine], st.at[mine], zhp)
    h_own("z", zp, slot(1, 0, 0), ALO)
    h_own("z", zp, slot(1, 0, 0), AHI)

    def near(dx, half, part, to):
        s = slot(0, 0, dx)
        got(("x", s, half))
        if to is not None:
            pass_on("x", to, s, slot(0, 0, 2), half)
        pass_on("z", zp, s, slot(1, 0, dx), part)
        pass_on("s", sib, s, slot(0, 1, dx), half)

    near(3, LO, ALO, xp)
    near(1, HI, AHI, xm)

    ring_on("g1zy", g1, 1 - zh, U // 2)
    ring("g2y", st.at[mine], st.at[mine])

    got(("z", slot(1, 0, 0), B))
    pass_on("x", xp, slot(1, 0, 0), slot(1, 0, 3), B)
    pass_on("x", xm, slot(1, 0, 0), slot(1, 0, 1), B)

    near(3, HI, AHI, None)
    near(1, LO, ALO, None)

    local[1].wait()
    got(("g1y", "pp"), ("g1y", "mm"), ("g1zy", "pp"), ("g1zy", "mm"))

    def feature_sums(n):
        at = pl.ds(pl.multiple_of(n * TILE, TILE), TILE)
        weight_tile(n).wait()
        p = lax.dot_general(
            g1[...].reshape(8 * U, M), wv[n % NW], (((1,), (1,)), ((), ())),
            preferred_element_type=F32,
        )
        own[:, at] = p[:T]
        for j in range(3):
            pb[j, :, at] = p[T * (j + 1) : T * (j + 2)].astype(BF16)

        @pl.when(n + NW < F // TILE)
        def _():
            weight_tile(n + NW).start()

    pl.loop(0, 7)(feature_sums)
    got("g2z")
    ring("g2zy", st.at[other], st.at[other])

    pl.loop(7, F // TILE)(feature_sums)

    lo, hi = pl.ds(0, HALF), pl.ds(HALF, HALF)
    early = len(copies)
    send("r1lo", pb.at[1, lo], r1.at[0], xm)
    send("r1hi", pb.at[1, hi], r1.at[1], xp)
    send("r2alo", pb.at[0, lo], r2.at[0, lo], xp)
    send("r2bhi", pb.at[2, hi], r2.at[1, hi], xm)

    ring_on("g2y", st, zh, 2)
    ring_on("g2zy", st, 1 - zh, 2)

    s = slot(0, 0, 2)
    for half in (LO, HI):
        got(("x", s, half))
        pass_on("s", sib, s, slot(0, 1, 2), half)
    for cols in COLS:
        for part in (ALO, AHI):
            pass_on("z", zp, s, slot(1, 0, 2), part, cols)

    got(("z", slot(1, 0, 0), ALO), ("z", slot(1, 0, 0), AHI))
    pass_on("s", sib, slot(1, 0, 0), slot(1, 1, 0), (0, T))

    got(("x", slot(1, 0, 3), B))
    pass_on("x", xp, slot(1, 0, 3), slot(1, 0, 2), BLO)
    got(("x", slot(1, 0, 1), B))
    pass_on("x", xm, slot(1, 0, 1), slot(1, 0, 2), BHI)

    got(("g2y", "pp"), ("g2y", "mm"), ("g2zy", "pp"), ("g2zy", "mm"))
    for dz in range(2):
        for dk in range(2):
            for dx in range(4):
                for half in range(2):
                    g2[slot(dz, dk, dx), half * U : (half + 1) * U, :] = st[(-dx if dk else dx) % 4 * 2 + half, dz * 2 + dk]

    def product(first, last, at):
        depth = (last - first) * T
        return lax.dot_general(
            hb[first:last, :, at].reshape(depth, TILE), g2[first:last].reshape(depth, SUB),
            (((0,), (0,)), ((), ())), preferred_element_type=F32,
        )

    local[0].wait()
    got(("s", slot(0, 1, 0), (0, T)))
    for dx in (1, 2, 3):
        got(("s", slot(0, 1, dx), LO), ("s", slot(0, 1, dx), HI))
    got(("s", slot(1, 1, 0), (0, T)))

    @pl.loop(0, F // TILE)
    def _(n):
        at = pl.ds(pl.multiple_of(n * TILE, TILE), TILE)
        acc[at, :] = product(0, 10, at)

    got("r1lo")
    pb[2, lo, :] = (pb[2, lo, :].astype(F32) + r1[0].astype(F32)).astype(BF16)
    send("r2blo", pb.at[2, lo], r2.at[1, lo], xm)
    got("r1hi")
    pb[0, hi, :] = (pb[0, hi, :].astype(F32) + r1[1].astype(F32)).astype(BF16)
    send("r2ahi", pb.at[0, hi], r2.at[0, hi], xp)

    for dx in (3, 1):
        got(("z", slot(1, 0, dx), ALO), ("z", slot(1, 0, dx), AHI))
        pass_on("s", sib, slot(1, 0, dx), slot(1, 1, dx), (0, T))

    sent(early)
    for i in range(1, 4):
        a2a[i].wait_send()

    @pl.when(jnp.logical_not(same))
    def _():
        a2a[0].wait_send()

    for dx in (1, 3):
        got(("s", slot(1, 1, dx), (0, T)))

    @pl.loop(0, F // TILE)
    def _(n):
        at = pl.ds(pl.multiple_of(n * TILE, TILE), TILE)
        acc[at, :] += product(10, 14, at)

    s = slot(1, 0, 2)
    for part in (BLO, BHI):
        got(("x", s, part))
        pass_on("s", sib, s, slot(1, 1, 2), part)
    for cols in COLS:
        for part in (ALO, AHI):
            got(("z", s, part, cols))
            pass_on("s", sib, s, slot(1, 1, 2), part, cols)
        if cols == COLS[0]:
            got(("s", slot(1, 1, 2), BLO), ("s", slot(1, 1, 2), BHI))
        if cols == COLS[1]:
            got("r2alo", "r2bhi")
            own[lo, :] += r2[0, lo, :].astype(F32)
            own[hi, :] += r2[1, hi, :].astype(F32)
        for part in (ALO, AHI):
            got(("s", slot(1, 1, 2), part, cols))

        @pl.loop(cols[0] // TILE, cols[1] // TILE)
        def _(n):
            at = pl.ds(pl.multiple_of(n * TILE, TILE), TILE)
            dw_ref[at, :] = ((acc[at, :] + product(14, 16, at)) * SCALE).astype(BF16)

    for i, (name, half) in enumerate((("r2blo", lo), ("r2ahi", hi))):
        got(name)
        hg_ref[half, :] = (own[half, :] + r2[1 - i, half, :].astype(F32)).astype(BF16)

    sent(len(copies))


def shards(hidden, grad_out, weight):
    hidden, grad_out, weight = (pltpu.with_memory_space_constraint(a, pltpu.HBM) for a in (hidden, grad_out, weight))
    return pl.pallas_call(
        kernel,
        out_shape=(jax.ShapeDtypeStruct((T, F), BF16), jax.ShapeDtypeStruct((F, SUB), BF16)),
        in_specs=[pl.BlockSpec(memory_space=pltpu.HBM)] * 3,
        out_specs=(pl.BlockSpec(memory_space=pltpu.VMEM), pl.BlockSpec(memory_space=pltpu.VMEM)),
        scratch_shapes=[
            pltpu.VMEM((16, T, F), BF16),
            pltpu.VMEM((NW, TILE, M), BF16),
            pltpu.VMEM((8, U, M), BF16),
            pltpu.VMEM((8, 4, U, SUB), BF16),
            pltpu.VMEM((16, T, SUB), BF16),
            pltpu.VMEM((T, F), F32),
            pltpu.VMEM((3, T, F), BF16),
            pltpu.VMEM((2, HALF, F), BF16),
            pltpu.VMEM((2, T, F), BF16),
            pltpu.VMEM((F, SUB), F32),
            pltpu.SemaphoreType.DMA((64,)),
            pltpu.SemaphoreType.DMA((64,)),
            pltpu.SemaphoreType.DMA((4,)),
            pltpu.SemaphoreType.DMA((4,)),
            pltpu.SemaphoreType.DMA((2,)),
            pltpu.SemaphoreType.DMA((NW,)),
        ],
        compiler_params=pltpu.CompilerParams(
            collective_id=0, has_side_effects=True, vmem_limit_bytes=44 * 2**20
        ),
        cost_estimate=pl.CostEstimate(
            flops=4 * 512 * M * F, bytes_accessed=2 * F * (M + SUB + 2 * T), transcendentals=0
        ),
    )(hidden, grad_out, weight)


def solution(mesh):
    return jax.shard_map(
        shards,
        mesh=mesh,
        in_specs=(P(("depth", "row"), "col"), P(("depth", "col"), "row"), P("col", "row")),
        out_specs=(P(("depth", "row"), "col"), P("col", ("depth", "row"))),
        check_vma=False,
    )
```

```python
import jax
import jax.numpy as jnp
from jax import lax
from jax.experimental import pallas as pl
from jax.experimental.pallas import tpu as pltpu
from jax.sharding import PartitionSpec as P

MESH = pl.DeviceIdType.MESH
BF16 = jnp.bfloat16
F32 = jnp.float32

T, F, U, M = 128, 3328, 64, 2048
SUB = M // 4
HALF = T // 2
TILE = 256
NW = 4
B_LO, B_HI = 16, 32
B0, B1 = HALF - B_LO, HALF + B_HI
LO, HI = (0, HALF), (HALF, T)
ALO, B, AHI = (0, B0), (B0, B1), (B1, T)
BLO, BHI = (B0, HALF), (HALF, B1)
COLS = ((0, 7 * TILE), (7 * TILE, F))
SCALE = 2048.0 ** -0.5


def slot(dz, dk, dx):
    return dk * 4 + dx if dz == 0 else 8 + (0, 1, 3, 2)[dx] * 2 + dk


def kernel(
    h_ref, g_ref, w_ref, hg_ref, dw_ref,
    hb, wv, g1, st, g2, own, pb, r1, r2, acc,
    ssem, rsem, a2s, a2r, lsem, wsem,
):
    d, r, c = lax.axis_index("depth"), lax.axis_index("row"), lax.axis_index("col")
    zl, k, zh, y = d // 2, d % 2, c // 4, c % 4
    xp, xm = (d, (r + 1 + 2 * k) % 4, c), (d, (r + 3 - 2 * k) % 4, c)
    zp, sib = ((1 - zl) * 2 + k, r, c), (zl * 2 + 1 - k, r, c)
    yp, ym = (d, r, zh * 4 + (y + 1) % 4), (d, r, zh * 4 + (y + 3) % 4)
    zhp = (d, r, (1 - zh) * 4 + y)

    def place(col, row, core):
        return ((1 + 2 * core) * (col // 2 + 4 - row) % 4) * 2 + col % 2

    mine, other = place(c, r, k), place((1 - zh) * 4 + y, r, k)
    same = d == r

    local = [
        pltpu.make_async_copy(h_ref, hb.at[slot(0, 0, 0)], lsem.at[0]),
        pltpu.make_async_copy(g_ref, g1.at[mine], lsem.at[1]),
    ]
    for cp in reversed(local):
        cp.start()

    def weight_tile(n):
        at = pl.ds(pl.multiple_of(n * TILE, TILE), TILE)
        return pltpu.make_async_copy(w_ref.at[at], wv.at[n % NW], wsem.at[n % NW])

    for n in range(NW):
        weight_tile(n).start()

    barrier = pltpu.get_barrier_semaphore()
    for who in (xp, xm, zp, sib, zhp, yp, ym):
        pl.semaphore_signal(barrier, inc=1, device_id=who, device_id_type=MESH)
    for i in range(4):
        source = ((d + i) % 4, d, c)
        if i == 0:
            @pl.when(jnp.logical_not(same))
            def _():
                pl.semaphore_signal(barrier, inc=1, device_id=source, device_id_type=MESH)
        else:
            pl.semaphore_signal(barrier, inc=1, device_id=source, device_id_type=MESH)
    pl.semaphore_wait(barrier, 11 - same.astype(jnp.int32))

    copies = {}

    def send(key, src, dst, to):
        n = len(copies)
        cp = pltpu.make_async_remote_copy(
            src_ref=src, dst_ref=dst, send_sem=ssem.at[n], recv_sem=rsem.at[n],
            device_id=to, device_id_type=MESH,
        )
        cp.start()
        copies[key] = cp

    done = []

    def sent(n):
        for cp in list(copies.values())[len(done) : n]:
            cp.wait_send()
            done.append(cp)

    def got(*keys):
        for key in keys:
            if isinstance(key, tuple) and len(key) == 3:
                key = (*key, (0, F))
            copies[key].wait_recv()

    def rows(s, span, cols=(0, F)):
        return hb.at[s, pl.ds(span[0], span[1] - span[0]), pl.ds(cols[0], cols[1] - cols[0])]

    def pass_on(name, to, src, dst, span, cols=(0, F)):
        send((name, dst, span, cols), rows(src, span, cols), rows(dst, span, cols), to)

    rel = ((zl + r // 2) % 2) * 2 + (k + r % 2) % 2
    a2a = []
    for i in range(4):
        j = (r + i) % 4
        src = g_ref.at[:, pl.ds(pl.multiple_of(j * SUB, SUB), SUB)]
        dst = st.at[place(c, j, r % 2), rel]
        cp = pltpu.make_async_remote_copy(
            src_ref=src, dst_ref=dst, send_sem=a2s.at[i], recv_sem=a2r.at[rel],
            device_id=(r, j, c), device_id_type=MESH,
        )
        a2a.append(cp)
        if i == 0:
            @pl.when(jnp.logical_not(same))
            def _():
                cp.start()

            @pl.when(same)
            def _():
                pltpu.make_async_copy(src, dst, a2r.at[0]).start()
        else:
            cp.start()

    def ring(name, src, dst):
        send((name, "p"), src, dst, yp)
        send((name, "m"), src, dst, ym)

    def ring_on(name, buf, layer, n):
        for way, off, at, to in (("p", 3, 0, yp), ("m", 1, n, ym)):
            part = buf.at[place(layer * 4 + (y + off) % 4, r, k), pl.ds(at, n)]
            got((name, way))
            send((name, 2 * way), part, part, to)

    send("g1z", g_ref, g1.at[mine], zhp)
    ring("g1y", g_ref, g1.at[mine])

    def h_own(name, to, dst, span):
        send((name, dst, span, (0, F)), h_ref.at[pl.ds(span[0], span[1] - span[0])], rows(dst, span), to)

    h_own("z", zp, slot(1, 0, 0), B)
    h_own("x", xp, slot(0, 0, 3), LO)
    h_own("x", xm, slot(0, 0, 1), HI)
    h_own("x", xp, slot(0, 0, 3), HI)
    h_own("x", xm, slot(0, 0, 1), LO)
    h_own("s", sib, slot(0, 1, 0), (0, T))

    got("g1z")
    ring("g1zy", g1.at[other], g1.at[other])
    ring_on("g1y", g1, zh, U // 2)

    for i in range(4):
        pltpu.make_async_copy(st.at[0, i], st.at[0, i], a2r.at[i]).wait()
    send("g2z", st.at[mine], st.at[mine], zhp)
    h_own("z", zp, slot(1, 0, 0), ALO)
    h_own("z", zp, slot(1, 0, 0), AHI)

    def near(dx, half, part, to):
        s = slot(0, 0, dx)
        got(("x", s, half))
        if to is not None:
            pass_on("x", to, s, slot(0, 0, 2), half)
        pass_on("z", zp, s, slot(1, 0, dx), part)
        pass_on("s", sib, s, slot(0, 1, dx), half)

    near(3, LO, ALO, xp)
    near(1, HI, AHI, xm)

    ring_on("g1zy", g1, 1 - zh, U // 2)
    ring("g2y", st.at[mine], st.at[mine])

    got(("z", slot(1, 0, 0), B))
    pass_on("x", xp, slot(1, 0, 0), slot(1, 0, 3), B)
    pass_on("x", xm, slot(1, 0, 0), slot(1, 0, 1), B)

    near(3, HI, AHI, None)
    near(1, LO, ALO, None)

    local[1].wait()
    got(("g1y", "pp"), ("g1y", "mm"), ("g1zy", "pp"), ("g1zy", "mm"))

    def feature_sums(n):
        at = pl.ds(pl.multiple_of(n * TILE, TILE), TILE)
        weight_tile(n).wait()
        p = lax.dot_general(
            g1[...].reshape(8 * U, M), wv[n % NW], (((1,), (1,)), ((), ())),
            preferred_element_type=F32,
        )
        own[:, at] = p[:T]
        for j in range(3):
            pb[j, :, at] = p[T * (j + 1) : T * (j + 2)].astype(BF16)

        @pl.when(n + NW < F // TILE)
        def _():
            weight_tile(n + NW).start()

    pl.loop(0, 7)(feature_sums)
    got("g2z")
    ring("g2zy", st.at[other], st.at[other])

    pl.loop(7, F // TILE)(feature_sums)

    lo, hi = pl.ds(0, HALF), pl.ds(HALF, HALF)
    early = len(copies)
    send("r1lo", pb.at[1, lo], r1.at[0], xm)
    send("r1hi", pb.at[1, hi], r1.at[1], xp)
    send("r2alo", pb.at[0, lo], r2.at[0, lo], xp)
    send("r2bhi", pb.at[2, hi], r2.at[1, hi], xm)

    ring_on("g2y", st, zh, 2)
    ring_on("g2zy", st, 1 - zh, 2)

    s = slot(0, 0, 2)
    for half in (LO, HI):
        got(("x", s, half))
        pass_on("s", sib, s, slot(0, 1, 2), half)
    for cols in COLS:
        for part in (ALO, AHI):
            pass_on("z", zp, s, slot(1, 0, 2), part, cols)

    got(("z", slot(1, 0, 0), ALO), ("z", slot(1, 0, 0), AHI))
    pass_on("s", sib, slot(1, 0, 0), slot(1, 1, 0), (0, T))

    got(("x", slot(1, 0, 3), B))
    pass_on("x", xp, slot(1, 0, 3), slot(1, 0, 2), BLO)
    got(("x", slot(1, 0, 1), B))
    pass_on("x", xm, slot(1, 0, 1), slot(1, 0, 2), BHI)

    got(("g2y", "pp"), ("g2y", "mm"), ("g2zy", "pp"), ("g2zy", "mm"))
    for dz in range(2):
        for dk in range(2):
            for dx in range(4):
                for half in range(2):
                    g2[slot(dz, dk, dx), half * U : (half + 1) * U, :] = st[(-dx if dk else dx) % 4 * 2 + half, dz * 2 + dk]

    def product(first, last, at):
        depth = (last - first) * T
        return lax.dot_general(
            hb[first:last, :, at].reshape(depth, TILE), g2[first:last].reshape(depth, SUB),
            (((0,), (0,)), ((), ())), preferred_element_type=F32,
        )

    local[0].wait()
    got(("s", slot(0, 1, 0), (0, T)))
    for dx in (1, 2, 3):
        got(("s", slot(0, 1, dx), LO), ("s", slot(0, 1, dx), HI))
    got(("s", slot(1, 1, 0), (0, T)))

    @pl.loop(0, F // TILE)
    def _(n):
        at = pl.ds(pl.multiple_of(n * TILE, TILE), TILE)
        acc[at, :] = product(0, 10, at)

    middle = len(copies)
    got("r1lo")
    pb[2, lo, :] = (pb[2, lo, :].astype(F32) + r1[0].astype(F32)).astype(BF16)
    send("r2blo", pb.at[2, lo], r2.at[1, lo], xm)
    got("r1hi")
    pb[0, hi, :] = (pb[0, hi, :].astype(F32) + r1[1].astype(F32)).astype(BF16)
    send("r2ahi", pb.at[0, hi], r2.at[0, hi], xp)

    for dx in (3, 1):
        got(("z", slot(1, 0, dx), ALO), ("z", slot(1, 0, dx), AHI))
        pass_on("s", sib, slot(1, 0, dx), slot(1, 1, dx), (0, T))

    sent(early)
    for i in range(1, 4):
        a2a[i].wait_send()

    @pl.when(jnp.logical_not(same))
    def _():
        a2a[0].wait_send()

    for dx in (1, 3):
        got(("s", slot(1, 1, dx), (0, T)))

    @pl.loop(0, F // TILE)
    def _(n):
        at = pl.ds(pl.multiple_of(n * TILE, TILE), TILE)
        acc[at, :] += product(10, 14, at)

    s = slot(1, 0, 2)
    for part in (BLO, BHI):
        got(("x", s, part))
        pass_on("s", sib, s, slot(1, 1, 2), part)
    for cols in COLS:
        for part in (ALO, AHI):
            got(("z", s, part, cols))
            pass_on("s", sib, s, slot(1, 1, 2), part, cols)
        if cols == COLS[0]:
            got(("s", slot(1, 1, 2), BLO), ("s", slot(1, 1, 2), BHI))
        if cols == COLS[1]:
            got("r2alo", "r2bhi")
            own[lo, :] += r2[0, lo, :].astype(F32)
            own[hi, :] += r2[1, hi, :].astype(F32)
            sent(middle)
        for part in (ALO, AHI):
            got(("s", slot(1, 1, 2), part, cols))

        @pl.loop(cols[0] // TILE, cols[1] // TILE)
        def _(n):
            at = pl.ds(pl.multiple_of(n * TILE, TILE), TILE)
            dw_ref[at, :] = ((acc[at, :] + product(14, 16, at)) * SCALE).astype(BF16)

    for i, (name, half) in enumerate((("r2blo", lo), ("r2ahi", hi))):
        got(name)
        hg_ref[half, :] = (own[half, :] + r2[1 - i, half, :].astype(F32)).astype(BF16)

    sent(len(copies))


def shards(hidden, grad_out, weight):
    hidden, grad_out, weight = (pltpu.with_memory_space_constraint(a, pltpu.HBM) for a in (hidden, grad_out, weight))
    return pl.pallas_call(
        kernel,
        out_shape=(jax.ShapeDtypeStruct((T, F), BF16), jax.ShapeDtypeStruct((F, SUB), BF16)),
        in_specs=[pl.BlockSpec(memory_space=pltpu.HBM)] * 3,
        out_specs=(pl.BlockSpec(memory_space=pltpu.VMEM), pl.BlockSpec(memory_space=pltpu.VMEM)),
        scratch_shapes=[
            pltpu.VMEM((16, T, F), BF16),
            pltpu.VMEM((NW, TILE, M), BF16),
            pltpu.VMEM((8, U, M), BF16),
            pltpu.VMEM((8, 4, U, SUB), BF16),
            pltpu.VMEM((16, T, SUB), BF16),
            pltpu.VMEM((T, F), F32),
            pltpu.VMEM((3, T, F), BF16),
            pltpu.VMEM((2, HALF, F), BF16),
            pltpu.VMEM((2, T, F), BF16),
            pltpu.VMEM((F, SUB), F32),
            pltpu.SemaphoreType.DMA((64,)),
            pltpu.SemaphoreType.DMA((64,)),
            pltpu.SemaphoreType.DMA((4,)),
            pltpu.SemaphoreType.DMA((4,)),
            pltpu.SemaphoreType.DMA((2,)),
            pltpu.SemaphoreType.DMA((NW,)),
        ],
        compiler_params=pltpu.CompilerParams(
            collective_id=0, has_side_effects=True, vmem_limit_bytes=44 * 2**20
        ),
        cost_estimate=pl.CostEstimate(
            flops=4 * 512 * M * F, bytes_accessed=2 * F * (M + SUB + 2 * T), transcendentals=0
        ),
    )(hidden, grad_out, weight)


def solution(mesh):
    return jax.shard_map(
        shards,
        mesh=mesh,
        in_specs=(P(("depth", "row"), "col"), P(("depth", "col"), "row"), P("col", "row")),
        out_specs=(P(("depth", "row"), "col"), P("col", ("depth", "row"))),
        check_vma=False,
    )
```
